32 devices in a mesh: inp: 2 (over x), tm: 16 (over z, y, core).
Axes of the slice: x: 2, y: 2, z: 4, core: 2. Of those that a mesh axis runs over, the one named last changes fastest.
Arguments:
- raw: bfloat16 [1024, 131072], P('inp', 'tm'), may hold values from -6 to 6
- taps: float32 [4, 512], replicated, may hold values from -3 to 3
Outputs:
- visibilities: float32 [256, 2, 1024, 1024], P('tm', None, 'inp')
The draws below stay inside these ranges and needn't reach their ends.
All inputs are finite; a program needn't handle non-finite values.
Results may differ from the reference program's by a relative error of at most 0.0052.
Values may be sent and summed in bfloat16 or wider, within the bound.
No kernel may reach another device: no remote copies, remote signals or barrier semaphores. Data moves between devices by JAX's collectives and lax.ppermute only.
A program may use at most 256 MiB of HBM per device.

```python
import math
import jax
import jax.numpy as jnp
from jax import lax

NI = 1024
NFFT = 512
TAPS = 4
NCH = 256
NSPEC = 256
NSAMP = 131072


def shard_levels(stream_key, dims, shards, smallest, top_value):
    def one(position, parts):
        draws = jax.random.uniform(jax.random.fold_in(jax.random.fold_in(stream_key, 6), position), (parts,), jnp.float32, smallest / len(shards), top_value / len(shards))
        return jnp.repeat(jnp.exp(draws), dims[position] // parts).reshape((-1,) + (1,) * (len(dims) - position - 1))

    level = one(*shards[0])
    for cut in shards[1:]:
        level = level * one(*cut)
    return level


def normal_values(stream_key, extent, spread, bound, cuts=(), held_as=jnp.bfloat16):
    array = jax.random.normal(stream_key, extent, jnp.float32) * spread
    if len(cuts) > 0:
        array = shard_levels(stream_key, extent, cuts, -0.22, 0.18) * array
    return jnp.clip(array, min=-bound, max=bound).astype(held_as)


def setup_inputs(seed: int = 0) -> dict:
    streams_of = jax.random.split(jax.random.key(seed), 3)
    return {
        "raw": normal_values(streams_of[0], (NI, NSAMP), 1.0, 6.0, ((0, 2), (1, 16))),
        "taps": normal_values(streams_of[1], (TAPS, NFFT), 0.5, 3.0, (), jnp.float32),
    }


def dft_table(length):
    half = length // 2
    kidx = jnp.arange(half, dtype=jnp.int32)[:, None]
    nidx = jnp.arange(length, dtype=jnp.int32)[None, :]
    phase = (kidx * nidx % length).astype(jnp.float32) * (2.0 * math.pi / length)
    norm = 1.0 / math.sqrt(length)
    return jnp.stack([jnp.cos(phase) * norm, -jnp.sin(phase) * norm], axis=1).astype(jnp.bfloat16)

def reference(raw, taps):
    blk = math.gcd(NI, 64)
    frames = raw.reshape(NI // blk, blk, NSPEC, NFFT)
    table = dft_table(NFFT).astype(jnp.float32)

    def engine(block):
        padded = jnp.concatenate([jnp.zeros((blk, TAPS - 1, NFFT), jnp.bfloat16), block], axis=1)
        filtered = sum((taps[t][None, None, :] * padded[:, t:t + NSPEC, :] for t in range(TAPS)))
        filtered = filtered.astype(jnp.bfloat16).astype(jnp.float32)
        return jnp.einsum('isn,crn->crsi', filtered, table).astype(jnp.bfloat16)
    pieces = lax.map(engine, frames)
    spectra = jnp.moveaxis(pieces, 0, 3).reshape(NCH, 2, NSPEC, NI)

    def tile(channel):
        values = channel.astype(jnp.float32)
        rotated = jnp.stack([values[1], -values[0]])
        real_part = jnp.einsum('rsi,rsj->ij', values, values)
        imag_part = jnp.einsum('rsi,rsj->ij', values, rotated)
        return jnp.stack([real_part, imag_part]) / NSPEC
    return lax.map(tile, spectra)
```

```python
import functools
import math

import jax
import jax.numpy as jnp
import numpy as np
from jax import lax
from jax.experimental import pallas as pl
from jax.experimental.pallas import tpu as pltpu
from jax.sharding import PartitionSpec as P

VMEM_LIMIT = 56 << 20


def after(value, earlier):
    return lax.optimization_barrier((value, *earlier))[0] if earlier else value


def from_behind(value, axis):
    devices = lax.axis_size(axis)
    return lax.ppermute(value, axis, [(i, i + 1) for i in range(devices - 1)])


def from_partner(value, axis):
    return lax.ppermute(value, axis, [(i, i ^ 1) for i in range(lax.axis_size(axis))])


def part_sizes(channels):
    part = max(1, channels // 4)
    return [part] * (channels // part) + [1] * (channels % part)


def dft_rows(length, devices, sizes):
    channels = length // 2
    own = channels // devices
    order = []
    first = 0
    for size in sizes:
        for owner in range(devices):
            order += range(owner * own + first, owner * own + first + size)
        first += size
    k = np.asarray(order)[:, None]
    phase = (k * np.arange(length)[None, :] % length) * (2.0 * math.pi / length)
    norm = 1.0 / math.sqrt(length)
    table = np.stack([np.cos(phase) * norm, -np.sin(phase) * norm], axis=1)
    return jnp.asarray(table.reshape(2 * channels, length), jnp.bfloat16)


def spectra_body(frames, length, group, taps_ref, table_ref, order_ref, raw_ref, halo_ref, *refs):
    *outs, scratch = refs
    n_taps = taps_ref.shape[0]
    taps = taps_ref[...]
    table = table_ref[...]

    def frame(f):
        ref, at = (halo_ref, f) if f < n_taps - 1 else (raw_ref, f - (n_taps - 1))
        return ref[:, at * length : (at + 1) * length].astype(jnp.float32)

    for s in range(frames):
        total = taps[0:1] * frame(s)
        for t in range(1, n_taps):
            total = total + taps[t : t + 1] * frame(s + t)
        spectrum = lax.dot_general(
            table,
            total.astype(jnp.bfloat16),
            (((1,), (1,)), ((), ())),
            preferred_element_type=jnp.float32,
        )
        scratch[s] = spectrum.astype(jnp.bfloat16)
    first = 0
    width = raw_ref.shape[0]
    for out in outs:
        for at in range(0, out.shape[0], group):
            mixed = scratch[:, first + at : first + at + group, :].reshape(group * frames, width)
            rows = jnp.dot(order_ref[...], mixed, preferred_element_type=jnp.float32)
            out[at : at + group] = rows.astype(jnp.bfloat16).reshape(group, frames, width)
        first += out.shape[0]


def make_spectra(raw, halo, taps, devices, sizes):
    n_taps, length = taps.shape
    inputs, samples = raw.shape
    frames = samples // length
    rows = length
    block = min(inputs, 256)
    group = 16
    order = np.zeros((group, frames, frames, group), np.float32)
    for r in range(group):
        for s in range(frames):
            order[r, s, s, r] = 1.0
    order = jnp.asarray(order.reshape(group * frames, group * frames), jnp.bfloat16)
    table = dft_rows(length, devices, sizes)
    counts = [devices * size * 2 for size in sizes]
    outs = pl.pallas_call(
        functools.partial(spectra_body, frames, length, group),
        grid=(inputs // block,),
        in_specs=[
            pl.BlockSpec(taps.shape, lambda i: (0, 0)),
            pl.BlockSpec(table.shape, lambda i: (0, 0)),
            pl.BlockSpec(order.shape, lambda i: (0, 0)),
            pl.BlockSpec((block, samples), lambda i: (i, 0)),
            pl.BlockSpec((block, halo.shape[1]), lambda i: (i, 0)),
        ],
        out_specs=[pl.BlockSpec((c, frames, block), lambda i: (0, 0, i)) for c in counts],
        out_shape=[jax.ShapeDtypeStruct((c, frames, inputs), jnp.bfloat16) for c in counts],
        scratch_shapes=[pltpu.VMEM((frames, rows, block), jnp.bfloat16)],
        compiler_params=pltpu.CompilerParams(vmem_limit_bytes=VMEM_LIMIT),
        cost_estimate=pl.CostEstimate(
            flops=2 * inputs * frames * rows * length,
            bytes_accessed=4 * inputs * samples,
            transcendentals=0,
        ),
        name="spectra",
    )(taps, table, order, raw, halo)
    return [
        out.reshape(devices, size, 2, frames, inputs) for out, size in zip(outs, sizes)
    ]


def correlate_body(count, group_ref, own_ref, other_ref, *refs):
    out_ref = refs[-1]
    sources, _, _, frames, inputs = own_ref.shape
    depth = sources * frames

    def parts(ref):
        return ref[:, 0, 0].reshape(depth, inputs), ref[:, 0, 1].reshape(depth, inputs)

    own = parts(own_ref)
    other = parts(other_ref)
    rows = jnp.transpose(jnp.concatenate(own, axis=0))

    def store(column, real, imag):
        where = slice(column, column + inputs)
        for which, pair in enumerate(((real, imag), (imag, -real))):
            product = jnp.dot(
                rows, jnp.concatenate(pair, axis=0), preferred_element_type=jnp.float32
            )
            out_ref[0, which, :, where] = product * (1.0 / count)

    @pl.when(group_ref[0] == 0)
    def _():
        store(0, *own)
        store(inputs, *other)

    @pl.when(group_ref[0] != 0)
    def _():
        store(inputs, *own)
        store(0, *other)


def correlate(group, own, other, earlier, shape, first, count):
    sources, channels, _, frames, inputs = own.shape
    held = [] if earlier is None else [earlier]
    spec = pl.BlockSpec((sources, 1, 2, frames, inputs), lambda c, g: (0, c, 0, 0, 0))
    return pl.pallas_call(
        functools.partial(correlate_body, count),
        grid_spec=pltpu.PrefetchScalarGridSpec(
            num_scalar_prefetch=1,
            grid=(channels,),
            in_specs=[spec, spec] + [pl.BlockSpec(memory_space=pl.ANY)] * len(held),
            out_specs=pl.BlockSpec(
                (1, 2, inputs, shape[3]), lambda c, g: (first + c, 0, 0, 0)
            ),
        ),
        out_shape=jax.ShapeDtypeStruct(shape, jnp.float32),
        input_output_aliases={3: 0} if held else {},
        compiler_params=pltpu.CompilerParams(vmem_limit_bytes=VMEM_LIMIT),
        cost_estimate=pl.CostEstimate(
            flops=channels * 16 * inputs * inputs * sources * frames,
            bytes_accessed=channels * 4 * inputs * (4 * inputs + 2 * sources * frames),
            transcendentals=0,
        ),
        name="correlate",
    )(group, own, other, *held)


def per_device(raw, taps):
    n_taps, length = taps.shape
    inputs, samples = raw.shape
    devices = lax.axis_size("tm")
    own_channels = length // 2 // devices
    count = samples // length * devices
    sizes = part_sizes(own_channels)
    halo = from_behind(raw[:, samples - (n_taps - 1) * length :], "tm")
    spectra = make_spectra(raw, halo, taps, devices, sizes)
    group = lax.axis_index("inp")[None]
    shape = (own_channels, 2, inputs, inputs * lax.axis_size("inp"))
    result = None
    turned, others = [], []
    for u, part in enumerate(spectra):
        part = after(part, others[u - 2 : u - 1] if u >= 2 else [])
        turned.append(lax.all_to_all(part, "tm", split_axis=0, concat_axis=0, tiled=True))
        others.append(from_partner(turned[u], "inp"))
    first = 0
    for size, own, other in zip(sizes, turned, others):
        result = correlate(group, own, other, result, shape, first, count)
        first += size
    return result


def solution(mesh):
    return jax.shard_map(
        per_device,
        mesh=mesh,
        in_specs=(P("inp", "tm"), P()),
        out_specs=P("tm", None, "inp", None),
        check_vma=False,
    )
```

```python
import functools
import math

import jax
import jax.numpy as jnp
import numpy as np
from jax import lax
from jax.experimental import pallas as pl
from jax.experimental.pallas import tpu as pltpu
from jax.sharding import PartitionSpec as P

VMEM_LIMIT = 56 << 20
HALVES = 2
CUT = 1
OWN_AT = 1
OTHER_AT = 4
FIRST = 2
XLAG = 3
ZORD = (1, 3, 2)
FAR = 3


def after(value, earlier):
    return lax.optimization_barrier((value, *earlier))[0] if earlier else value


def from_behind(value, axis):
    devices = lax.axis_size(axis)
    return lax.ppermute(value, axis, [(i, i + 1) for i in range(devices - 1)])


def from_partner(value, axis, by):
    return lax.ppermute(value, axis, [(i, i ^ by) for i in range(lax.axis_size(axis))])


def dft_rows(length, devices, halves):
    channels = length // 2
    part = channels // devices // halves
    k = np.arange(channels).reshape(devices, halves, part).transpose(1, 0, 2)[..., None]
    phase = (k * np.arange(length) % length) * (2.0 * math.pi / length)
    norm = 1.0 / math.sqrt(length)
    table = np.stack([np.cos(phase) * norm, -np.sin(phase) * norm], axis=3)
    return jnp.asarray(table.reshape(halves, devices, 2 * part, length), jnp.bfloat16)


def filtered(taps, frame, s):
    total = taps[0:1] * frame(s)
    for t in range(1, taps.shape[0]):
        total = total + taps[t : t + 1] * frame(s + t)
    return total.astype(jnp.bfloat16)


def transform(table, values):
    return lax.dot_general(
        table, values, (((1,), (1,)), ((), ())), preferred_element_type=jnp.float32
    ).astype(jnp.bfloat16)


def place_table(here_ref, table_ref, table):
    halves, devices, rows, _ = table_ref.shape

    @pl.when(pl.program_id(0) == 0)
    def _():
        for h in range(halves):
            for d in range(devices):
                at = (h * devices + d) * rows
                table[at : at + rows] = table_ref[h, here_ref[0] ^ d]


def late_body(here_ref, taps_ref, table_ref, raw_ref, out_ref, table):
    length = taps_ref.shape[1]
    taps = taps_ref[...]
    place_table(here_ref, table_ref, table)

    def frame(f):
        return raw_ref[:, f * length : (f + 1) * length].astype(jnp.float32)

    for s in range(out_ref.shape[0]):
        out_ref[s] = transform(table[...], filtered(taps, frame, s))


def pieces_body(group, here_ref, taps_ref, table_ref, order_ref, late_ref, raw_ref, halo_ref, *refs):
    *outs, table = refs
    n_taps, length = taps_ref.shape
    width = raw_ref.shape[0]
    early = n_taps - 1
    frames = early + late_ref.shape[0]
    rows = table_ref.shape[2]
    taps = taps_ref[...]
    place_table(here_ref, table_ref, table)

    def frame(f):
        ref, at = (halo_ref, f) if f < early else (raw_ref, f - early)
        return ref[:, at * length : (at + 1) * length].astype(jnp.float32)

    first_ones = [transform(table[...], filtered(taps, frame, s)) for s in range(early)]
    for first in range(0, table.shape[0], group):
        mixed = [one[first : first + group] for one in first_ones]
        mixed += [late_ref[s, first : first + group] for s in range(frames - early)]
        turned = jnp.dot(
            order_ref[...], jnp.concatenate(mixed, axis=0), preferred_element_type=jnp.float32
        )
        turned = turned.astype(jnp.bfloat16).reshape(group, frames, width)
        step = min(group, rows)
        for at in range(0, group, step):
            piece, row = divmod(first + at, rows)
            outs[piece][row // 2 : (row + step) // 2] = turned[at : at + step].reshape(
                step // 2, 2, frames, width
            )


def late_spectra(here, raw, taps, table, frames):
    n_taps, length = taps.shape
    inputs, samples = raw.shape
    block = min(inputs, 256)
    late = frames - (n_taps - 1)
    return pl.pallas_call(
        late_body,
        grid_spec=pltpu.PrefetchScalarGridSpec(
            num_scalar_prefetch=1,
            grid=(inputs // block,),
            in_specs=[
                pl.BlockSpec(taps.shape, lambda i, t: (0, 0)),
                pl.BlockSpec(table.shape, lambda i, t: (0, 0, 0, 0)),
                pl.BlockSpec((block, samples), lambda i, t: (i, 0)),
            ],
            out_specs=pl.BlockSpec((late, length, block), lambda i, t: (0, 0, i)),
            scratch_shapes=[pltpu.VMEM((length, length), jnp.bfloat16)],
        ),
        out_shape=jax.ShapeDtypeStruct((late, length, inputs), jnp.bfloat16),
        compiler_params=pltpu.CompilerParams(vmem_limit_bytes=VMEM_LIMIT),
        cost_estimate=pl.CostEstimate(
            flops=2 * inputs * samples * length, bytes_accessed=4 * inputs * samples, transcendentals=0
        ),
        name="late_spectra",
    )(here, taps, table, raw)


def make_pieces(h, here, late, raw, halo, taps, table):
    halves, devices, rows, length = table.shape
    inputs = raw.shape[0]
    frames = late.shape[0] + taps.shape[0] - 1
    block = min(inputs, 256)
    group = 16
    order = np.zeros((group, frames, frames, group), np.float32)
    for r in range(group):
        for s in range(frames):
            order[r, s, s, r] = 1.0
    order = jnp.asarray(order.reshape(group * frames, group * frames), jnp.bfloat16)
    edge = pl.BlockSpec((block, halo.shape[1]), lambda i, t: (i, 0))
    outs = pl.pallas_call(
        functools.partial(pieces_body, group),
        grid_spec=pltpu.PrefetchScalarGridSpec(
            num_scalar_prefetch=1,
            grid=(inputs // block,),
            in_specs=[
                pl.BlockSpec(taps.shape, lambda i, t: (0, 0)),
                pl.BlockSpec((1, devices, rows, length), lambda i, t: (h, 0, 0, 0)),
                pl.BlockSpec(order.shape, lambda i, t: (0, 0)),
                pl.BlockSpec((late.shape[0], devices * rows, block), lambda i, t: (0, h, i)),
                edge,
                edge,
            ],
            out_specs=[
                pl.BlockSpec((rows // 2, 2, frames, block), lambda i, t: (0, 0, 0, i))
            ] * devices,
            scratch_shapes=[pltpu.VMEM((devices * rows, length), jnp.bfloat16)],
        ),
        out_shape=[jax.ShapeDtypeStruct((rows // 2, 2, frames, inputs), jnp.bfloat16)] * devices,
        compiler_params=pltpu.CompilerParams(vmem_limit_bytes=VMEM_LIMIT),
        cost_estimate=pl.CostEstimate(
            flops=4 * inputs * frames * devices * rows * group * frames // 2,
            bytes_accessed=4 * inputs * frames * devices * rows,
            transcendentals=0,
        ),
        name="pieces",
    )(here, taps, table, order, late, raw, halo)
    return dict(enumerate(outs))


def correlate_body(count, n, crossed, group_ref, *refs):
    out_ref, token_ref = refs[-2:]
    frames, inputs = refs[0].shape[2:]

    def parts(pieces):
        return [
            jnp.concatenate([piece[0, r] for piece in pieces], axis=0) for r in range(2)
        ]

    own = parts(refs[:n])
    real, imag = parts(refs[n : 2 * n]) if crossed else own
    rows = jnp.transpose(jnp.concatenate(own, axis=0))
    for which, pair in enumerate(((real, imag), (imag, -real))):
        product = jnp.dot(rows, jnp.concatenate(pair, axis=0), preferred_element_type=jnp.float32)
        out_ref[0, which] = product * (1.0 / count)
    token_ref[...] = jnp.zeros_like(token_ref)


def correlate(group, own, other, earlier, shape, first, start, channels, count):
    n = len(own)
    _, _, frames, inputs = own[0].shape
    pieces = own + (other or [])
    held = [] if earlier is None else [earlier]
    crossed = other is not None
    spec = pl.BlockSpec((1, 2, frames, inputs), lambda c, g: (start + c, 0, 0, 0))
    return pl.pallas_call(
        functools.partial(correlate_body, count, n, crossed),
        grid_spec=pltpu.PrefetchScalarGridSpec(
            num_scalar_prefetch=1,
            grid=(channels,),
            in_specs=[spec] * len(pieces) + [pl.BlockSpec(memory_space=pl.ANY)] * len(held),
            out_specs=[
                pl.BlockSpec(
                    (1, 2, inputs, inputs),
                    lambda c, g: (first + start + c, 0, 0, 1 - g[0] if crossed else g[0]),
                ),
                pl.BlockSpec((8, 128), lambda c, g: (0, 0)),
            ],
        ),
        out_shape=[
            jax.ShapeDtypeStruct(shape, jnp.float32),
            jax.ShapeDtypeStruct((8, 128), jnp.float32),
        ],
        input_output_aliases={1 + len(pieces): 0} if held else {},
        compiler_params=pltpu.CompilerParams(vmem_limit_bytes=VMEM_LIMIT),
        cost_estimate=pl.CostEstimate(
            flops=channels * 8 * inputs * inputs * n * frames,
            bytes_accessed=channels * 4 * inputs * (2 * inputs + 2 * n * frames),
            transcendentals=0,
        ),
        name="correlate_other" if crossed else "correlate_own",
    )(group, *pieces, *held)


def turn_orders(devices):
    near = max(1, devices // 4)
    far = [q + near * z for q in range(near) for z in ZORD if q + near * z < devices]
    close = list(range(1, near))
    return far, close, list(range(near)) + far


def per_device(raw, taps):
    n_taps, length = taps.shape
    inputs, samples = raw.shape
    devices = lax.axis_size("tm")
    own_channels = length // 2 // devices
    count = samples // length * devices
    halves = HALVES if own_channels % HALVES == 0 else 1
    part = own_channels // halves
    halo = from_behind(raw[:, samples - (n_taps - 1) * length :], "tm")
    here = lax.axis_index("tm")[None]
    table = dft_rows(length, devices, halves)
    late = late_spectra(here, raw, taps, table, samples // length)
    group = lax.axis_index("inp")[None]
    shape = (own_channels, 2, inputs, inputs * lax.axis_size("inp"))

    far, close, order = turn_orders(devices)
    come, others, tokens = {}, {}, []
    far_chain, close_chain, chain = [], [], []
    result = None

    def send(key, value, sent, lag, axis, by, arrived, more=()):
        earlier = [arrived[sent[-lag]]] if len(sent) >= lag else []
        arrived[key] = from_partner(after(value, earlier + list(more)), axis, by)
        sent.append(key)

    for h in range(halves):
        wait = [others[0, order[0]]] if h else []
        spectra = make_pieces(h, here, after(late, wait), raw, halo, taps, table)
        come[h, 0] = spectra[0]
        if not h:
            send((h, 0), come[h, 0], chain, XLAG, "inp", 1, others)
        for k, d in enumerate(far):
            more = [others[0, 0]] if FIRST == k and not h else []
            send((h, d), spectra[d], far_chain, FAR, "tm", d, come, more)
        for d in close:
            send((h, d), spectra[d], close_chain, 1, "tm", d, come)
        for k, d in enumerate(order):
            if (h, d) in others:
                continue
            more = [token for at, token in zip((OWN_AT, OTHER_AT), tokens) if at == k]
            send((h, d), come[h, d], chain, XLAG, "inp", 1, others, more)
        own = [come[h, d] for d in range(devices)]
        other = [others[h, d] for d in range(devices)]
        tokens = []
        cut = max(1, part // CUT)
        for crossed in (None, other):
            for start in range(0, part, cut):
                result, token = correlate(
                    group, own, crossed, result, shape, h * part, start, min(cut, part - start), count
                )
                tokens.append(token)
    return result


def solution(mesh):
    return jax.shard_map(
        per_device,
        mesh=mesh,
        in_specs=(P("inp", "tm"), P()),
        out_specs=P("tm", None, "inp", None),
        check_vma=False,
    )
```

```python
import functools
import math

import jax
import jax.numpy as jnp
import numpy as np
from jax import lax
from jax.experimental import pallas as pl
from jax.experimental.pallas import tpu as pltpu
from jax.sharding import PartitionSpec as P

VMEM_LIMIT = 56 << 20
HALVES = 2
FIRST = 2
XLAG = 3
ZORD = (1, 3, 2)
FAR = 3


def after(value, earlier):
    return lax.optimization_barrier((value, *earlier))[0] if earlier else value


def from_behind(value, axis):
    devices = lax.axis_size(axis)
    return lax.ppermute(value, axis, [(i, i + 1) for i in range(devices - 1)])


def from_partner(value, axis, by):
    return lax.ppermute(value, axis, [(i, i ^ by) for i in range(lax.axis_size(axis))])


def dft_rows(length, devices, halves):
    channels = length // 2
    part = channels // devices // halves
    k = np.arange(channels).reshape(devices, halves, part).transpose(1, 0, 2)[..., None]
    phase = (k * np.arange(length) % length) * (2.0 * math.pi / length)
    norm = 1.0 / math.sqrt(length)
    table = np.stack([np.cos(phase) * norm, -np.sin(phase) * norm], axis=3)
    return jnp.asarray(table.reshape(halves, devices, 2 * part, length), jnp.bfloat16)


def filtered(taps, frame, s):
    total = taps[0:1] * frame(s)
    for t in range(1, taps.shape[0]):
        total = total + taps[t : t + 1] * frame(s + t)
    return total.astype(jnp.bfloat16)


def transform(table, values):
    return lax.dot_general(
        table, values, (((1,), (1,)), ((), ())), preferred_element_type=jnp.float32
    ).astype(jnp.bfloat16)


def place_table(here_ref, table_ref, table):
    halves, devices, rows, _ = table_ref.shape

    @pl.when(pl.program_id(0) == 0)
    def _():
        for h in range(halves):
            for d in range(devices):
                at = (h * devices + d) * rows
                table[at : at + rows] = table_ref[h, here_ref[0] ^ d]


def late_body(here_ref, taps_ref, table_ref, raw_ref, out_ref, table):
    length = taps_ref.shape[1]
    taps = taps_ref[...]
    place_table(here_ref, table_ref, table)

    def frame(f):
        return raw_ref[:, f * length : (f + 1) * length].astype(jnp.float32)

    for s in range(out_ref.shape[0]):
        out_ref[s] = transform(table[...], filtered(taps, frame, s))


def pieces_body(group, here_ref, taps_ref, table_ref, order_ref, late_ref, raw_ref, halo_ref, *refs):
    *outs, table = refs
    n_taps, length = taps_ref.shape
    width = raw_ref.shape[0]
    early = n_taps - 1
    frames = early + late_ref.shape[0]
    rows = table_ref.shape[2]
    taps = taps_ref[...]
    place_table(here_ref, table_ref, table)

    def frame(f):
        ref, at = (halo_ref, f) if f < early else (raw_ref, f - early)
        return ref[:, at * length : (at + 1) * length].astype(jnp.float32)

    first_ones = [transform(table[...], filtered(taps, frame, s)) for s in range(early)]
    for first in range(0, table.shape[0], group):
        mixed = [one[first : first + group] for one in first_ones]
        mixed += [late_ref[s, first : first + group] for s in range(frames - early)]
        turned = jnp.dot(
            order_ref[...], jnp.concatenate(mixed, axis=0), preferred_element_type=jnp.float32
        )
        turned = turned.astype(jnp.bfloat16).reshape(group, frames, width)
        step = min(group, rows)
        for at in range(0, group, step):
            piece, row = divmod(first + at, rows)
            outs[piece][row // 2 : (row + step) // 2] = turned[at : at + step].reshape(
                step // 2, 2, frames, width
            )


def late_spectra(here, raw, taps, table, frames):
    n_taps, length = taps.shape
    inputs, samples = raw.shape
    block = min(inputs, 256)
    late = frames - (n_taps - 1)
    return pl.pallas_call(
        late_body,
        grid_spec=pltpu.PrefetchScalarGridSpec(
            num_scalar_prefetch=1,
            grid=(inputs // block,),
            in_specs=[
                pl.BlockSpec(taps.shape, lambda i, t: (0, 0)),
                pl.BlockSpec(table.shape, lambda i, t: (0, 0, 0, 0)),
                pl.BlockSpec((block, samples), lambda i, t: (i, 0)),
            ],
            out_specs=pl.BlockSpec((late, length, block), lambda i, t: (0, 0, i)),
            scratch_shapes=[pltpu.VMEM((length, length), jnp.bfloat16)],
        ),
        out_shape=jax.ShapeDtypeStruct((late, length, inputs), jnp.bfloat16),
        compiler_params=pltpu.CompilerParams(vmem_limit_bytes=VMEM_LIMIT),
        cost_estimate=pl.CostEstimate(
            flops=2 * inputs * samples * length, bytes_accessed=4 * inputs * samples, transcendentals=0
        ),
        name="late_spectra",
    )(here, taps, table, raw)


def make_pieces(h, here, late, raw, halo, taps, table):
    halves, devices, rows, length = table.shape
    inputs = raw.shape[0]
    frames = late.shape[0] + taps.shape[0] - 1
    block = min(inputs, 256)
    group = 16
    order = np.zeros((group, frames, frames, group), np.float32)
    for r in range(group):
        for s in range(frames):
            order[r, s, s, r] = 1.0
    order = jnp.asarray(order.reshape(group * frames, group * frames), jnp.bfloat16)
    edge = pl.BlockSpec((block, halo.shape[1]), lambda i, t: (i, 0))
    outs = pl.pallas_call(
        functools.partial(pieces_body, group),
        grid_spec=pltpu.PrefetchScalarGridSpec(
            num_scalar_prefetch=1,
            grid=(inputs // block,),
            in_specs=[
                pl.BlockSpec(taps.shape, lambda i, t: (0, 0)),
                pl.BlockSpec((1, devices, rows, length), lambda i, t: (h, 0, 0, 0)),
                pl.BlockSpec(order.shape, lambda i, t: (0, 0)),
                pl.BlockSpec((late.shape[0], devices * rows, block), lambda i, t: (0, h, i)),
                edge,
                edge,
            ],
            out_specs=[
                pl.BlockSpec((rows // 2, 2, frames, block), lambda i, t: (0, 0, 0, i))
            ] * devices,
            scratch_shapes=[pltpu.VMEM((devices * rows, length), jnp.bfloat16)],
        ),
        out_shape=[jax.ShapeDtypeStruct((rows // 2, 2, frames, inputs), jnp.bfloat16)] * devices,
        compiler_params=pltpu.CompilerParams(vmem_limit_bytes=VMEM_LIMIT),
        cost_estimate=pl.CostEstimate(
            flops=4 * inputs * frames * devices * rows * group * frames // 2,
            bytes_accessed=4 * inputs * frames * devices * rows,
            transcendentals=0,
        ),
        name="pieces",
    )(here, taps, table, order, late, raw, halo)
    return dict(enumerate(outs))


def stacked(pieces):
    return [jnp.concatenate([piece[0, r] for piece in pieces], axis=0) for r in range(2)]


def products(count, rows, real, imag, out_ref):
    for which, pair in enumerate(((real, imag), (imag, -real))):
        product = jnp.dot(rows, jnp.concatenate(pair, axis=0), preferred_element_type=jnp.float32)
        out_ref[0, which] = product * (1.0 / count)


def own_body(count, n, group_ref, *refs):
    out_ref, rows_ref = refs[-2:]
    real, imag = stacked(refs[:n])
    rows = jnp.transpose(jnp.concatenate([real, imag], axis=0))
    rows_ref[0] = rows
    products(count, rows, real, imag, out_ref)


def other_body(count, n, group_ref, rows_ref, *refs):
    real, imag = stacked(refs[:n])
    products(count, rows_ref[0], real, imag, refs[-1])


def correlate(group, rows, pieces, earlier, shape, first, count):
    n = len(pieces)
    channels, _, frames, inputs = pieces[0].shape
    depth = 2 * n * frames
    crossed = rows is not None
    before = [rows] if crossed else []
    held = [] if earlier is None else [earlier]
    spec = pl.BlockSpec((1, 2, frames, inputs), lambda c, g: (c, 0, 0, 0))
    rows_spec = pl.BlockSpec((1, inputs, depth), lambda c, g: (c, 0, 0))
    out_spec = pl.BlockSpec(
        (1, 2, inputs, inputs), lambda c, g: (first + c, 0, 0, 1 - g[0] if crossed else g[0])
    )
    out_shape = jax.ShapeDtypeStruct(shape, jnp.float32)
    rows_shape = jax.ShapeDtypeStruct((channels, inputs, depth), jnp.bfloat16)
    outs = pl.pallas_call(
        functools.partial(other_body if crossed else own_body, count, n),
        grid_spec=pltpu.PrefetchScalarGridSpec(
            num_scalar_prefetch=1,
            grid=(channels,),
            in_specs=[rows_spec] * len(before)
            + [spec] * n
            + [pl.BlockSpec(memory_space=pl.ANY)] * len(held),
            out_specs=[out_spec] if crossed else [out_spec, rows_spec],
        ),
        out_shape=[out_shape] if crossed else [out_shape, rows_shape],
        input_output_aliases={1 + len(before) + n: 0} if held else {},
        compiler_params=pltpu.CompilerParams(vmem_limit_bytes=VMEM_LIMIT),
        cost_estimate=pl.CostEstimate(
            flops=channels * 4 * inputs * inputs * depth,
            bytes_accessed=channels * 4 * inputs * (2 * inputs + depth),
            transcendentals=0,
        ),
        name="correlate_other" if crossed else "correlate_own",
    )(group, *before, *pieces, *held)
    return outs[0], rows if crossed else outs[1]


def turn_orders(devices):
    near = max(1, devices // 4)
    far = [q + near * z for q in range(near) for z in ZORD if q + near * z < devices]
    close = list(range(1, near))
    return far, close, list(range(near)) + far


def per_device(raw, taps):
    n_taps, length = taps.shape
    inputs, samples = raw.shape
    devices = lax.axis_size("tm")
    own_channels = length // 2 // devices
    count = samples // length * devices
    halves = HALVES if own_channels % HALVES == 0 else 1
    part = own_channels // halves
    halo = from_behind(raw[:, samples - (n_taps - 1) * length :], "tm")
    here = lax.axis_index("tm")[None]
    table = dft_rows(length, devices, halves)
    late = late_spectra(here, raw, taps, table, samples // length)
    group = lax.axis_index("inp")[None]
    shape = (own_channels, 2, inputs, inputs * lax.axis_size("inp"))

    far, close, order = turn_orders(devices)
    come, others = {}, {}
    far_chain, close_chain, chain = [], [], []
    result = None

    def send(key, value, sent, lag, axis, by, arrived, more=()):
        earlier = [arrived[sent[-lag]]] if len(sent) >= lag else []
        arrived[key] = from_partner(after(value, earlier + list(more)), axis, by)
        sent.append(key)

    for h in range(halves):
        wait = [others[0, order[0]]] if h else []
        spectra = make_pieces(h, here, after(late, wait), raw, halo, taps, table)
        come[h, 0] = spectra[0]
        if not h:
            send((h, 0), come[h, 0], chain, XLAG, "inp", 1, others)
        for k, d in enumerate(far):
            more = [others[0, 0]] if FIRST == k and not h else []
            send((h, d), spectra[d], far_chain, FAR, "tm", d, come, more)
        for d in close:
            send((h, d), spectra[d], close_chain, 1, "tm", d, come)
        for k, d in enumerate(order):
            if (h, d) in others:
                continue
            send((h, d), come[h, d], chain, XLAG, "inp", 1, others)
        own = [come[h, d] for d in range(devices)]
        other = [others[h, d] for d in range(devices)]
        result, rows = correlate(group, None, own, result, shape, h * part, count)
        result, _ = correlate(group, rows, other, result, shape, h * part, count)
    return result


def solution(mesh):
    return jax.shard_map(
        per_device,
        mesh=mesh,
        in_specs=(P("inp", "tm"), P()),
        out_specs=P("tm", None, "inp", None),
        check_vma=False,
    )
```
